512 devices in a mesh: seq: 16 (over z_lo, y), col: 32 (over z_hi, x, core).
Axes of the slice: x: 4, y: 4, z: 16 (z_hi: 4, z_lo: 4; z = z_hi * 4 + z_lo), core: 2. Of those that a mesh axis runs over, the one named last changes fastest.
Arguments:
- layer_in: bfloat16 [512, 256, 768], P('seq', 'col'), may hold values from -13.5 to 13.5
- cotangent: bfloat16 [512, 256, 768], P('seq', 'col'), may hold values from -6 to 6
- w_query: bfloat16 [768, 384], replicated, may hold values from -0.21875 to 0.21875
- w_key: bfloat16 [768, 384], replicated, may hold values from -0.21875 to 0.21875
- w_value: bfloat16 [768, 384], replicated, may hold values from -0.21875 to 0.21875
- w_out: bfloat16 [384, 768], replicated, may hold values from -0.3125 to 0.3125
Outputs:
- layer_out: bfloat16 [512, 256, 768], P('seq', 'col')
- input_grad: bfloat16 [512, 256, 768], P('seq', 'col')
The draws below stay inside these ranges and needn't reach their ends.
All inputs are finite; a program needn't handle non-finite values.
Results may differ from the reference program's by a relative error of at most 0.025.
Values may be sent and summed in bfloat16 or wider, within the bound.
No kernel may reach another device: no remote copies, remote signals or barrier semaphores. Data moves between devices by JAX's collectives and lax.ppermute only.
A program may use at most 64 MiB of HBM per device.

```python
import math
import jax
import jax.numpy as jnp
from jax import lax

D = 768
H = 6
DH = 64
HD = 384
R_DEV = 32
C_DEV = 8
ROWS = 512
COLS = 256


def draw_layer_in(key, part):
    key = jax.random.fold_in(key, 7)
    noise_key, pair_key = jax.random.split(key, 2)
    block_count = COLS // C_DEV
    row_block = jnp.arange(ROWS, dtype=jnp.int32) // R_DEV
    col_block = jnp.arange(COLS, dtype=jnp.int32) // C_DEV
    partner = jax.random.permutation(pair_key, block_count)[row_block % block_count]
    spike_scale = jnp.where(partner[:, None] == col_block[None, :], 3.0, 1.0).astype(jnp.float32)
    noise_field = jax.random.truncated_normal(noise_key, -4.5, 4.5, (ROWS, COLS, D), jnp.float32)
    drawn_field = spike_scale[:, :, None] * noise_field
    return drawn_field.astype(jnp.bfloat16)


def block_levels(own_key, extent, cuts, low, largest):
    loudness, own = 1.0, jax.random.fold_in(own_key, 6)
    for position, shards_of in cuts:
        draws = jnp.exp(jax.random.uniform(jax.random.fold_in(own, position), (shards_of,), jnp.float32, low / len(cuts), largest / len(cuts)))
        loudness = loudness * jnp.repeat(draws, extent[position] // shards_of).reshape([-1 if axis == position else 1 for axis in range(len(extent))])
    return loudness


def scatter_about(stream_key, shape, deviation, limit, shards=(), held_as=jnp.bfloat16):
    drawn = jax.random.normal(stream_key, shape, jnp.float32) * deviation
    if len(shards) > 0:
        drawn = block_levels(stream_key, shape, shards, -0.22, 0.18) * drawn
    return jnp.clip(drawn, min=-limit, max=limit).astype(held_as)


def setup_inputs(seed: int = 0) -> dict:
    keys = jax.random.split(jax.random.key(seed), 7)
    layer_in = draw_layer_in(jax.random.fold_in(keys[6], 71), 0)
    cotangent = scatter_about(keys[1], (ROWS, COLS, D), 1.0, 6.0, ((0, 16), (1, 32)))
    w_query = scatter_about(keys[2], (D, HD), D ** -0.5, 0.21875)
    w_key = scatter_about(keys[3], (D, HD), D ** -0.5, 0.21875)
    w_value = scatter_about(keys[4], (D, HD), D ** -0.5, 0.21875)
    w_out = scatter_about(keys[5], (HD, D), HD ** -0.5, 0.3125)
    return {"layer_in": layer_in, "cotangent": cotangent, "w_query": w_query, "w_key": w_key, "w_value": w_value, "w_out": w_out}


def reference(layer_in, cotangent, w_query, w_key, w_value, w_out):
    row_count, col_count, feature = layer_in.shape
    flattened = layer_in.reshape(row_count * col_count, feature)

    def project(weight):
        result = jnp.dot(flattened, weight, preferred_element_type=jnp.float32).astype(jnp.bfloat16)
        return result.reshape(row_count, col_count, H, DH).astype(jnp.float32)
    queries = project(w_query)
    keys_all = project(w_key)
    values = project(w_value)
    scaling = 1.0 / math.sqrt(DH * ROWS)
    logits = jnp.einsum('rihe,rjhe->hij', queries, keys_all) * scaling
    attn_probs = jax.nn.softmax(logits, axis=-1).astype(jnp.bfloat16)
    prob_f32 = attn_probs.astype(jnp.float32)
    attended = jnp.einsum('hij,rjhe->rihe', prob_f32, values).astype(jnp.bfloat16)
    attended = attended.reshape(row_count * col_count, H * DH)
    layer_out = jnp.dot(attended, w_out, preferred_element_type=jnp.float32).astype(jnp.bfloat16)
    layer_out = layer_out.reshape(row_count, col_count, feature)
    d_att = lax.dot_general(cotangent.reshape(-1, feature), w_out, (((1,), (1,)), ((), ())), preferred_element_type=jnp.float32).astype(jnp.bfloat16)
    d_att = d_att.reshape(row_count, col_count, H, DH).astype(jnp.float32)
    d_prob = jnp.einsum('rihe,rjhe->hij', d_att, values)
    d_logit = prob_f32 * (d_prob - lax.optimization_barrier(jnp.sum(prob_f32 * d_prob, axis=-1, keepdims=True))) * scaling
    d_logit = d_logit.astype(jnp.bfloat16).astype(jnp.float32)
    d_query = jnp.einsum('hij,rjhe->rihe', d_logit, keys_all).astype(jnp.bfloat16)
    d_key = jnp.einsum('hij,rihe->rjhe', d_logit, queries).astype(jnp.bfloat16)
    d_value = jnp.einsum('hij,rihe->rjhe', prob_f32, d_att).astype(jnp.bfloat16)
    gradients = jnp.concatenate((d_query.reshape(-1, H * DH), d_key.reshape(-1, H * DH), d_value.reshape(-1, H * DH)), axis=1)
    stacked = jnp.concatenate((w_query, w_key, w_value), axis=1)
    input_grad = lax.dot_general(gradients, stacked, (((1,), (1,)), ((), ())), preferred_element_type=jnp.float32).astype(jnp.bfloat16)
    return (layer_out, input_grad.reshape(row_count, col_count, feature))
```

```python
import math

import jax
import jax.numpy as jnp
import numpy as np
from jax import lax
from jax.experimental import pallas as pl
from jax.experimental.pallas import tpu as pltpu
from jax.sharding import Mesh, PartitionSpec as P

H = 6
DH = 64
HD = H * DH
D = 768
NT = 32
RE = 512
SCALING = 1.0 / math.sqrt(DH * 512)
X = ("x1", "x0")
I_PAIRS = [(0, 1), (1, 0), (2, 3), (3, 2)]
J_PAIRS = [(0, 3), (3, 0), (1, 2), (2, 1)]
BF = jnp.bfloat16
F32 = jnp.float32


def dot(a, b):
    return jnp.dot(a, b, preferred_element_type=F32)


def dot_t(a, b):
    return lax.dot_general(a, b, (((1,), (1,)), ((), ())), preferred_element_type=F32)


def low_half(shape):
    return lax.broadcasted_iota(jnp.int32, shape, len(shape) - 1) < DH


def roll_half(tile):
    flat = tile.reshape(-1, 2 * DH)
    return pltpu.roll(flat, DH, 1).reshape(tile.shape)


def tokens_to_heads(tokens, put):
    split = tokens.reshape(4, 4, 2, 8, HD)
    keep = low_half((4, 4, 8, 128))
    for tile in range(3):
        first = split[:, :, 0, :, tile * 128 : tile * 128 + 128]
        second = split[:, :, 1, :, tile * 128 : tile * 128 + 128]
        even = jnp.where(keep, first, roll_half(second))
        odd = jnp.where(keep, roll_half(first), second)
        for pair in range(4):
            put(2 * tile, pair, even[:, pair].reshape(NT, 128))
            put(2 * tile + 1, pair, odd[:, pair].reshape(NT, 128))


def heads_to_tokens(heads, scratch):
    keep = low_half((NT, 128))
    for tile in range(3):
        even, odd = heads(2 * tile), heads(2 * tile + 1)
        for pair in range(4):
            a = even[:, pair * 128 : pair * 128 + 128]
            b = odd[:, pair * 128 : pair * 128 + 128]
            first = jnp.where(keep, a, roll_half(b))
            second = jnp.where(keep, roll_half(a), b)
            lanes = slice(tile * 128, tile * 128 + 128)
            scratch[:, 2 * pair, :, lanes] = first.reshape(4, 8, 128)
            scratch[:, 2 * pair + 1, :, lanes] = second.reshape(4, 8, 128)


def call(body, out_shape, scratch=(), flops=0, data=0, scalars=0, inputs=1):
    return pl.pallas_call(
        body,
        out_shape=out_shape,
        in_specs=[pl.BlockSpec(memory_space=pltpu.SMEM)] * scalars
        + [pl.BlockSpec(memory_space=pltpu.VMEM)] * inputs,
        out_specs=jax.tree.map(lambda _: pl.BlockSpec(memory_space=pltpu.VMEM), out_shape),
        scratch_shapes=list(scratch),
        compiler_params=pltpu.CompilerParams(vmem_limit_bytes=40 * 2**20),
        cost_estimate=pl.CostEstimate(flops=flops, bytes_accessed=data, transcendentals=0),
    )


def shaped(shape, dtype):
    return jax.ShapeDtypeStruct(shape, dtype)


def project_body(x_ref, wq_ref, wk_ref, wv_ref, q_ref, kv_ref):
    x = x_ref[...]

    def put_q(h, pair, block):
        q_ref[h, :, pair * 128 : pair * 128 + 128] = block.astype(BF)

    def put_kv(which):
        def put(h, pair, block):
            kv_ref[which, h, :, pair * 128 : pair * 128 + 128] = block.astype(BF)

        return put

    tokens_to_heads(dot(x, wq_ref[...]), put_q)
    tokens_to_heads(dot(x, wk_ref[...]), put_kv(0))
    tokens_to_heads(dot(x, wv_ref[...]), put_kv(1))


def relayout_body(a_ref, out_ref):
    def put(h, pair, block):
        out_ref[h, :, pair * 128 : pair * 128 + 128] = block.astype(BF)

    tokens_to_heads(a_ref[...].astype(F32), put)


def partial_body(par_ref, q, qo, da, dao, kv, kvo, kvc, out_ref, scr):
    par = par_ref[0]
    for h in range(H):
        for which, own, other in ((0, q, qo), (1, da, dao)):
            left = jnp.concatenate([own[h], other[h]], axis=0)
            right = jnp.concatenate([kv[which, h], kvo[which, h], kvc[0, which, h], kvc[1, which, h]], axis=0)
            part = dot_t(left, right)
            rows = slice((which * 3 + h % 3) * 8, (which * 3 + h % 3) * 8 + 8)
            for side in range(2):
                place = lax.bitwise_xor(par, side) * 8 + h // 3
                for zs in range(4):
                    start = side * NT + zs * 8
                    scr[place + 2 * zs, rows, :] = part[start : start + 8]
    out_ref[...] = scr[...].astype(BF)


def sum_body(a_ref, out_ref):
    total = a_ref[0].astype(F32)
    for k in range(1, 16):
        total = total + a_ref[k].astype(F32)
    for k in range(8):
        out_ref[k] = total


def softmax_body(par_ref, g_ref, out_ref):
    total = g_ref[0:2] + g_ref[2:4] + g_ref[4:6] + g_ref[6:8]
    own_first = par_ref[0] == 0
    l0, l1 = total[0, 0:24] * SCALING, total[1, 0:24] * SCALING
    d0, d1 = total[0, 24:48], total[1, 24:48]
    top = jnp.maximum(jnp.max(l0, axis=-1, keepdims=True), jnp.max(l1, axis=-1, keepdims=True))
    e0, e1 = jnp.exp(l0 - top), jnp.exp(l1 - top)
    norm = jnp.sum(e0, axis=-1, keepdims=True) + jnp.sum(e1, axis=-1, keepdims=True)
    p0 = (e0 / norm).astype(BF).astype(F32)
    p1 = (e1 / norm).astype(BF).astype(F32)
    mean = jnp.sum(p0 * d0, axis=-1, keepdims=True) + jnp.sum(p1 * d1, axis=-1, keepdims=True)
    prob = jnp.where(own_first, p0, p1)
    d_prob = jnp.where(own_first, d0, d1)
    d_logit = prob * (d_prob - mean) * SCALING
    both = jnp.concatenate([prob, d_logit], axis=0).astype(BF)
    for k in range(16):
        out_ref[k] = both


def mix_body(par_ref, pd_ref, q, qo, da, dao, kv, kvo, kvc, i_own, i_send, j_own, j_x, j_core, scr):
    par = par_ref[0]
    scr[...] = pd_ref[...].astype(F32)
    for h in range(H):
        probs, d_logits = [], []
        for side in range(2):
            place = lax.bitwise_xor(par, side) * 8 + h // 3
            for zs in range(4):
                probs.append(scr[place + 2 * zs, (h % 3) * 8 : (h % 3) * 8 + 8, :])
                d_logits.append(scr[place + 2 * zs, 24 + (h % 3) * 8 : 24 + (h % 3) * 8 + 8, :])
        prob = jnp.concatenate(probs, axis=0)
        d_logit = jnp.concatenate(d_logits, axis=0)
        keys = jnp.concatenate([kv[0, h], kvo[0, h], kvc[0, 0, h], kvc[1, 0, h]], axis=0)
        values = jnp.concatenate([kv[1, h], kvo[1, h], kvc[0, 1, h], kvc[1, 1, h]], axis=0)
        queries = jnp.concatenate([q[h], qo[h]], axis=0)
        d_att = jnp.concatenate([da[h], dao[h]], axis=0)
        attended = dot(prob.astype(BF), values)
        d_query = dot(d_logit.astype(BF), keys)
        d_key = dot(d_logit.T.astype(BF), queries)
        d_value = dot(prob.T.astype(BF), d_att)
        for which, value in ((0, attended), (1, d_query)):
            i_own[which, h] = value[0:NT]
            i_send[which, h] = value[NT:].astype(BF)
        for which, value in ((0, d_key), (1, d_value)):
            j_own[which, h] = value[0:NT]
            j_x[which, h] = value[NT : 2 * NT]
            j_core[0, which, h] = value[2 * NT : 3 * NT].astype(BF)
            j_core[1, which, h] = value[3 * NT :].astype(BF)


def add_body(j_x, j_core, out_ref):
    out_ref[...] = (j_x[...] + j_core[1].astype(F32)).astype(BF)


def finish_body(i_own, i_recv, j_own, j_core, j_recv, wq_ref, wk_ref, wv_ref, att_ref, grad_ref, scr):
    def gather(heads):
        heads_to_tokens(heads, scr)
        return scr[...].reshape(4 * 8 * 8, HD).astype(BF)

    att_ref[...] = gather(lambda h: i_own[0, h] + i_recv[0, h].astype(F32))
    d_query = gather(lambda h: i_own[1, h] + i_recv[1, h].astype(F32))
    total = dot_t(d_query, wq_ref[...])
    for which, weight in ((0, wk_ref), (1, wv_ref)):
        grad = gather(
            lambda h: j_own[which, h] + j_core[0, which, h].astype(F32) + j_recv[which, h].astype(F32)
        )
        total = total + dot_t(grad, weight[...])
    grad_ref[...] = total.astype(BF)


def shards(layer_in, cotangent, w_query, w_key, w_value, w_out):
    par = lax.axis_index("x0").astype(jnp.int32).reshape(1)
    units = (H, NT, RE)

    def over_z_hi(a):
        return lax.all_to_all(a, "zh", split_axis=0, concat_axis=0, tiled=True)

    with jax.named_scope("layer_in_to_home"):
        x_home = over_z_hi(layer_in).reshape(256, D)
    with jax.named_scope("d_att"):
        d_att = dot_t(cotangent.reshape(256, D), w_out).astype(BF).reshape(32, 8, HD)
        d_att = over_z_hi(d_att).reshape(256, HD)
    with jax.named_scope("project"):
        q, kv = call(
            project_body, (shaped(units, BF), shaped((2,) + units, BF)), flops=2 * 256 * D * 3 * HD, data=3 * 2**20, inputs=4
        )(x_home, w_query, w_key, w_value)
        da = call(relayout_body, shaped(units, BF), data=2**19)(d_att)
    with jax.named_scope("exchange_blocks"):
        qo = lax.ppermute(q, X, I_PAIRS)
        kvo = lax.ppermute(kv, X, J_PAIRS)
        dao = lax.ppermute(da, X, I_PAIRS)
        kvc = lax.ppermute(jnp.stack([kv, kvo]), "core", [(0, 1), (1, 0)])
    with jax.named_scope("partial_sums"):
        part = call(
            partial_body, shaped((16, 48, 128), BF), [pltpu.VMEM((16, 48, 128), F32)],
            flops=2 * 2 * H * 64 * 128 * RE, data=2**21, scalars=1, inputs=7,
        )(par, q, qo, da, dao, kv, kvo, kvc)
    with jax.named_scope("reduce"):
        part = lax.all_to_all(part, ("zh", "zl"), split_axis=0, concat_axis=0, tiled=True)
        part = call(sum_body, shaped((8, 48, 128), F32), data=2**19)(part)
        part = lax.all_to_all(part, ("y", "x0"), split_axis=0, concat_axis=0, tiled=True)
        both = call(softmax_body, shaped((16, 48, 128), BF), data=2**19, scalars=1)(par, part)
        both = lax.all_to_all(both, ("zh", "zl"), split_axis=0, concat_axis=0, tiled=True)
    with jax.named_scope("mix"):
        i_own, i_send, j_own, j_x, j_core = call(
            mix_body,
            (
                shaped((2,) + units, F32), shaped((2,) + units, BF), shaped((2,) + units, F32),
                shaped((2,) + units, F32), shaped((2, 2) + units, BF),
            ),
            [pltpu.VMEM((16, 48, 128), F32)], flops=4 * 2 * H * 64 * 128 * RE, data=2**22, scalars=1, inputs=8,
        )(par, both, q, qo, da, dao, kv, kvo, kvc)
    with jax.named_scope("exchange_sums"):
        i_recv = lax.ppermute(i_send, X, I_PAIRS)
        j_core = lax.ppermute(j_core, "core", [(0, 1), (1, 0)])
        j_send = call(add_body, shaped((2,) + units, BF), data=2**20, inputs=2)(j_x, j_core)
        j_recv = lax.ppermute(j_send, X, J_PAIRS)
    with jax.named_scope("finish"):
        attended, grad = call(
            finish_body, (shaped((256, HD), BF), shaped((256, D), BF)), [pltpu.VMEM((4, 8, 8, HD), F32)],
            flops=2 * 256 * D * 3 * HD, data=2**22, inputs=8,
        )(i_own, i_recv, j_own, j_core, j_recv, w_query, w_key, w_value)
    with jax.named_scope("to_owners"):
        attended = over_z_hi(attended.reshape(32, 8, HD)).reshape(256, HD)
        layer_out = dot(attended, w_out).astype(BF).reshape(32, 8, D)
        grad = over_z_hi(grad.reshape(32, 8, D))
    return (layer_out, grad)


def solution(mesh):
    fine = Mesh(np.asarray(mesh.devices).reshape(4, 4, 4, 2, 2, 2), ("zl", "y", "zh", "x1", "x0", "core"))
    tokens = P(("zl", "y"), ("zh", "x1", "x0", "core"), None)
    return jax.shard_map(
        shards,
        mesh=fine,
        in_specs=(tokens, tokens, P(), P(), P(), P()),
        out_specs=(tokens, tokens),
        check_vma=False,
    )
```

```python
import math

import jax
import jax.numpy as jnp
import numpy as np
from jax import lax
from jax.experimental import pallas as pl
from jax.experimental.pallas import tpu as pltpu
from jax.sharding import Mesh, PartitionSpec as P

H = 6
DH = 64
HD = H * DH
D = 768
NT = 32
RE = 512
SCALING = 1.0 / math.sqrt(DH * 512)
Z = ("z1", "z0")
I_PAIRS = [(0, 1), (1, 0), (2, 3), (3, 2)]
J_PAIRS = [(0, 3), (3, 0), (1, 2), (2, 1)]
BF = jnp.bfloat16
F32 = jnp.float32


def dot(a, b):
    return jnp.dot(a, b, preferred_element_type=F32)


def dot_t(a, b):
    return lax.dot_general(a, b, (((1,), (1,)), ((), ())), preferred_element_type=F32)


def low_half(shape):
    return lax.broadcasted_iota(jnp.int32, shape, len(shape) - 1) < DH


def roll_half(tile):
    flat = tile.reshape(-1, 2 * DH)
    return pltpu.roll(flat, DH, 1).reshape(tile.shape)


def tokens_to_heads(tokens, put):
    split = tokens.reshape(4, 4, 2, 8, HD)
    keep = low_half((4, 4, 8, 128))
    for tile in range(3):
        first = split[:, :, 0, :, tile * 128 : tile * 128 + 128]
        second = split[:, :, 1, :, tile * 128 : tile * 128 + 128]
        even = jnp.where(keep, first, roll_half(second))
        odd = jnp.where(keep, roll_half(first), second)
        for pair in range(4):
            put(2 * tile, pair, even[:, pair].reshape(NT, 128))
            put(2 * tile + 1, pair, odd[:, pair].reshape(NT, 128))


def heads_to_tokens(heads, scratch):
    keep = low_half((NT, 128))
    for tile in range(3):
        even, odd = heads(2 * tile), heads(2 * tile + 1)
        for pair in range(4):
            a = even[:, pair * 128 : pair * 128 + 128]
            b = odd[:, pair * 128 : pair * 128 + 128]
            first = jnp.where(keep, a, roll_half(b))
            second = jnp.where(keep, roll_half(a), b)
            lanes = slice(tile * 128, tile * 128 + 128)
            scratch[:, 2 * pair, :, lanes] = first.reshape(4, 8, 128)
            scratch[:, 2 * pair + 1, :, lanes] = second.reshape(4, 8, 128)


def call(body, out_shape, scratch=(), flops=0, data=0, scalars=0, inputs=1):
    return pl.pallas_call(
        body,
        out_shape=out_shape,
        in_specs=[pl.BlockSpec(memory_space=pltpu.SMEM)] * scalars
        + [pl.BlockSpec(memory_space=pltpu.VMEM)] * inputs,
        out_specs=jax.tree.map(lambda _: pl.BlockSpec(memory_space=pltpu.VMEM), out_shape),
        scratch_shapes=list(scratch),
        compiler_params=pltpu.CompilerParams(vmem_limit_bytes=40 * 2**20),
        cost_estimate=pl.CostEstimate(flops=flops, bytes_accessed=data, transcendentals=0),
    )


def shaped(shape, dtype):
    return jax.ShapeDtypeStruct(shape, dtype)


def project_body(home_ref, wq_ref, wk_ref, wv_ref, q_ref, kv_ref, da_ref):
    x = home_ref[:, 0:D]

    def put_q(h, pair, block):
        q_ref[h, :, pair * 128 : pair * 128 + 128] = block.astype(BF)

    def put_kv(which):
        def put(h, pair, block):
            kv_ref[which, h, :, pair * 128 : pair * 128 + 128] = block.astype(BF)

        return put

    tokens_to_heads(dot(x, wq_ref[...]), put_q)
    tokens_to_heads(dot(x, wk_ref[...]), put_kv(0))
    tokens_to_heads(dot(x, wv_ref[...]), put_kv(1))

    def put_da(h, pair, block):
        da_ref[h, :, pair * 128 : pair * 128 + 128] = block.astype(BF)

    tokens_to_heads(home_ref[:, D:].astype(F32), put_da)


def partial_body(par_ref, q, qo, da, dao, kv, kvo, kvc, out_ref, scr):
    par = par_ref[0]
    for h in range(H):
        for which, own, other in ((0, q, qo), (1, da, dao)):
            left = jnp.concatenate([own[h], other[h]], axis=0)
            right = jnp.concatenate([kv[which, h], kvo[which, h], kvc[0, which, h], kvc[1, which, h]], axis=0)
            part = dot_t(left, right)
            rows = slice((which * 3 + h % 3) * 8, (which * 3 + h % 3) * 8 + 8)
            for side in range(2):
                place = lax.bitwise_xor(par, side) * 8 + h // 3
                for xs in range(4):
                    start = side * NT + xs * 8
                    scr[place + 2 * xs, rows, :] = part[start : start + 8]
    out_ref[...] = scr[...].astype(BF)


def sum_body(a_ref, out_ref):
    total = a_ref[0].astype(F32)
    for k in range(1, 16):
        total = total + a_ref[k].astype(F32)
    for k in range(8):
        out_ref[k] = total


def softmax_body(par_ref, g_ref, out_ref):
    total = g_ref[0:2] + g_ref[2:4] + g_ref[4:6] + g_ref[6:8]
    own_first = par_ref[0] == 0
    l0, l1 = total[0, 0:24] * SCALING, total[1, 0:24] * SCALING
    d0, d1 = total[0, 24:48], total[1, 24:48]
    top = jnp.maximum(jnp.max(l0, axis=-1, keepdims=True), jnp.max(l1, axis=-1, keepdims=True))
    e0, e1 = jnp.exp(l0 - top), jnp.exp(l1 - top)
    norm = jnp.sum(e0, axis=-1, keepdims=True) + jnp.sum(e1, axis=-1, keepdims=True)
    p0 = (e0 / norm).astype(BF).astype(F32)
    p1 = (e1 / norm).astype(BF).astype(F32)
    mean = jnp.sum(p0 * d0, axis=-1, keepdims=True) + jnp.sum(p1 * d1, axis=-1, keepdims=True)
    prob = jnp.where(own_first, p0, p1)
    d_prob = jnp.where(own_first, d0, d1)
    d_logit = prob * (d_prob - mean) * SCALING
    both = jnp.concatenate([prob, d_logit], axis=0).astype(BF)
    for k in range(16):
        out_ref[k] = both


def mix_body(par_ref, pd_ref, q, qo, da, dao, kv, kvo, kvc, i_own, i_send, j_own, j_z, j_core, scr):
    par = par_ref[0]
    scr[...] = pd_ref[...].astype(F32)
    for h in range(H):
        probs, d_logits = [], []
        for side in range(2):
            place = lax.bitwise_xor(par, side) * 8 + h // 3
            for xs in range(4):
                probs.append(scr[place + 2 * xs, (h % 3) * 8 : (h % 3) * 8 + 8, :])
                d_logits.append(scr[place + 2 * xs, 24 + (h % 3) * 8 : 24 + (h % 3) * 8 + 8, :])
        prob = jnp.concatenate(probs, axis=0)
        d_logit = jnp.concatenate(d_logits, axis=0)
        keys = jnp.concatenate([kv[0, h], kvo[0, h], kvc[0, 0, h], kvc[1, 0, h]], axis=0)
        values = jnp.concatenate([kv[1, h], kvo[1, h], kvc[0, 1, h], kvc[1, 1, h]], axis=0)
        queries = jnp.concatenate([q[h], qo[h]], axis=0)
        d_att = jnp.concatenate([da[h], dao[h]], axis=0)
        attended = dot(prob.astype(BF), values)
        d_query = dot(d_logit.astype(BF), keys)
        d_key = dot(d_logit.T.astype(BF), queries)
        d_value = dot(prob.T.astype(BF), d_att)
        for which, value in ((0, attended), (1, d_query)):
            i_own[which, h] = value[0:NT]
            i_send[which, h] = value[NT:].astype(BF)
        for which, value in ((0, d_key), (1, d_value)):
            j_own[which, h] = value[0:NT]
            j_z[which, h] = value[NT : 2 * NT]
            j_core[0, which, h] = value[2 * NT : 3 * NT].astype(BF)
            j_core[1, which, h] = value[3 * NT :].astype(BF)


def add_body(j_z, j_core, out_ref):
    out_ref[...] = (j_z[...] + j_core[1].astype(F32)).astype(BF)


def finish_body(i_own, i_recv, j_own, j_core, j_recv, wq_ref, wk_ref, wv_ref, out_ref, scr):
    def gather(heads):
        heads_to_tokens(heads, scr)
        return scr[...].reshape(4 * 8 * 8, HD).astype(BF)

    out_ref[:, D:] = gather(lambda h: i_own[0, h] + i_recv[0, h].astype(F32))
    d_query = gather(lambda h: i_own[1, h] + i_recv[1, h].astype(F32))
    total = dot_t(d_query, wq_ref[...])
    for which, weight in ((0, wk_ref), (1, wv_ref)):
        grad = gather(
            lambda h: j_own[which, h] + j_core[0, which, h].astype(F32) + j_recv[which, h].astype(F32)
        )
        total = total + dot_t(grad, weight[...])
    out_ref[:, 0:D] = total.astype(BF)


def shards(layer_in, cotangent, w_query, w_key, w_value, w_out):
    par = lax.axis_index("z0").astype(jnp.int32).reshape(1)
    units = (H, NT, RE)

    def over_x(a):
        return lax.all_to_all(a, "x", split_axis=0, concat_axis=0, tiled=True)

    with jax.named_scope("to_homes"):
        d_att = dot_t(cotangent.reshape(256, D), w_out).astype(BF).reshape(32, 8, HD)
        home = over_x(jnp.concatenate([layer_in, d_att], axis=2)).reshape(256, D + HD)
    with jax.named_scope("project"):
        q, kv, da = call(
            project_body, (shaped(units, BF), shaped((2,) + units, BF), shaped(units, BF)),
            flops=2 * 256 * D * 3 * HD, data=3 * 2**20, inputs=4,
        )(home, w_query, w_key, w_value)
    with jax.named_scope("exchange_blocks"):
        qo = lax.ppermute(q, Z, I_PAIRS)
        kvo = lax.ppermute(kv, Z, J_PAIRS)
        dao = lax.ppermute(da, Z, I_PAIRS)
        kvc = lax.ppermute(jnp.stack([kv, kvo]), "core", [(0, 1), (1, 0)])
    with jax.named_scope("partial_sums"):
        part = call(
            partial_body, shaped((16, 48, 128), BF), [pltpu.VMEM((16, 48, 128), F32)],
            flops=2 * 2 * H * 64 * 128 * RE, data=2**21, scalars=1, inputs=7,
        )(par, q, qo, da, dao, kv, kvo, kvc)
    with jax.named_scope("reduce"):
        part = lax.all_to_all(part, ("y", "x"), split_axis=0, concat_axis=0, tiled=True)
        part = call(sum_body, shaped((8, 48, 128), F32), data=2**19)(part)
        part = lax.all_to_all(part, ("zl", "z0"), split_axis=0, concat_axis=0, tiled=True)
        both = call(softmax_body, shaped((16, 48, 128), BF), data=2**19, scalars=1)(par, part)
        both = lax.all_to_all(both, ("y", "x"), split_axis=0, concat_axis=0, tiled=True)
    with jax.named_scope("mix"):
        i_own, i_send, j_own, j_z, j_core = call(
            mix_body,
            (
                shaped((2,) + units, F32), shaped((2,) + units, BF), shaped((2,) + units, F32),
                shaped((2,) + units, F32), shaped((2, 2) + units, BF),
            ),
            [pltpu.VMEM((16, 48, 128), F32)], flops=4 * 2 * H * 64 * 128 * RE, data=2**22, scalars=1, inputs=8,
        )(par, both, q, qo, da, dao, kv, kvo, kvc)
    with jax.named_scope("exchange_sums"):
        i_recv = lax.ppermute(i_send, Z, I_PAIRS)
        j_core = lax.ppermute(j_core, "core", [(0, 1), (1, 0)])
        j_send = call(add_body, shaped((2,) + units, BF), data=2**20, inputs=2)(j_z, j_core)
        j_recv = lax.ppermute(j_send, Z, J_PAIRS)
    with jax.named_scope("finish"):
        home = call(
            finish_body, shaped((256, D + HD), BF), [pltpu.VMEM((4, 8, 8, HD), F32)],
            flops=2 * 256 * D * 3 * HD, data=2**22, inputs=8,
        )(i_own, i_recv, j_own, j_core, j_recv, w_query, w_key, w_value)
    with jax.named_scope("to_owners"):
        home = over_x(home.reshape(32, 8, D + HD))
        layer_out = dot(home[:, :, D:].reshape(256, HD), w_out).astype(BF).reshape(32, 8, D)
        grad = home[:, :, 0:D]
    return (layer_out, grad)


def solution(mesh):
    fine = Mesh(np.asarray(mesh.devices).reshape(4, 4, 2, 2, 4, 2), ("zl", "y", "z1", "z0", "x", "core"))
    tokens = P(("zl", "y"), ("z1", "z0", "x", "core"), None)
    return jax.shard_map(
        shards,
        mesh=fine,
        in_specs=(tokens, tokens, P(), P(), P(), P()),
        out_specs=(tokens, tokens),
        check_vma=False,
    )
```
